32 devices in a mesh: grp: 2 (over y), inp: 4 (over x, core), out: 4 (over z).
Axes of the slice: x: 2, y: 2, z: 4, core: 2. Of those that a mesh axis runs over, the one named last changes fastest.
Arguments:
- saved_inputs: bfloat16 [6, 128, 28672], P('grp', 'inp', 'out'), parts along dimension 0, may hold values from -6 to 6
- output_grads: bfloat16 [6, 128, 8192], P('grp', 'out', 'inp'), parts along dimension 0, may hold values from -6 to 6
- lengths: int32 [6], P('grp'), parts along dimension 0, may hold values from 1 to 128
- keep_mask: int32 [6, 128], P('grp'), parts along dimension 0, may hold values 0 or 1
- basis_in: bfloat16 [28672, 14336], P('out', 'inp'), may hold values from -0.03125 to 0.03125
- basis_out: bfloat16 [8192, 4096], P('inp', 'out'), may hold values from -0.0625 to 0.0625
Outputs:
- correction: float32 [8192, 14336], P(('grp', 'out'), 'inp'), parts along dimension 0
The draws below stay inside these ranges and needn't reach their ends.
There are 2 independent parts, one for each index of `grp`. The reference program is written for one: setup_inputs(seed, part) draws one part's arguments, and reference() takes and returns one part's arrays. A program takes and returns all parts, laid end to end along the dimension named above; an argument that names none is the same for every part. Nothing has to cross between parts.
All inputs are finite; a program needn't handle non-finite values.
Results may differ from the reference program's by a relative error of at most 0.0043.
Values may be sent and summed in bfloat16 or wider, within the bound.
A program may use at most 192 MiB of HBM per device.

```python
import jax
import jax.numpy as jnp

D_IN = 28672
D_OUT = 8192
KA = 14336
KG = 4096
SEQS = 3
LEN = 128


def with_ends(entries, rng, low, high):
    longest = entries.shape.index(max(entries.shape))
    spots = []
    for shift in (0, 1):
        where = [jax.random.randint(jax.random.fold_in(rng, axis), (), 0, length) for axis, length in enumerate(entries.shape)]
        where[longest] = (where[longest] + shift) % entries.shape[longest]
        spots.append(tuple(where))
    return entries.at[spots[0]].set(low).at[spots[1]].set(high)


def shard_levels(stream_key, shape, cuts, low, top_value):
    level, own = 1.0, jax.random.fold_in(stream_key, 6)
    for dim, parts in cuts:
        steps = jnp.exp(jax.random.uniform(jax.random.fold_in(own, dim), (parts,), jnp.float32, low / len(cuts), top_value / len(cuts)))
        level = level * jnp.repeat(steps, shape[dim] // parts).reshape([-1 if axis == dim else 1 for axis in range(len(shape))])
    return level


def bell_draw(own_key, extent, deviation, bound, cuts=(), kind=jnp.bfloat16):
    values = jax.random.normal(own_key, extent, jnp.float32) * deviation
    if len(cuts) > 0:
        values = shard_levels(own_key, extent, cuts, -0.22, 0.18) * values
    return jnp.clip(values, min=-bound, max=bound).astype(kind)


def setup_inputs(seed: int = 0, part: int = 0) -> dict:
    seeds = jax.random.split(jax.random.key(seed), 7)
    part_keys = jax.random.split(jax.random.fold_in(seeds[6], part), 7)
    return {
        "saved_inputs": bell_draw(part_keys[0], (SEQS, LEN, D_IN), 1.0, 6.0, ((1, 4), (2, 4))),
        "output_grads": bell_draw(part_keys[1], (SEQS, LEN, D_OUT), 1.0, 6.0, ((1, 4), (2, 4))),
        "lengths": jax.random.randint(part_keys[2], (SEQS,), 1, LEN + 1).astype(jnp.int32),
        "keep_mask": with_ends((jax.random.randint(part_keys[3], (SEQS, LEN), 0, 4) < 3).astype(jnp.int32), jax.random.fold_in(part_keys[3], 1), 0, 1),
        "basis_in": bell_draw(seeds[4], (D_IN, KA), D_IN ** -0.5, 0.03125, ((0, 4), (1, 4))),
        "basis_out": bell_draw(seeds[5], (D_OUT, KG), D_OUT ** -0.5, 0.0625, ((0, 4), (1, 4))),
    }


def reference(saved_inputs, output_grads, lengths, keep_mask, basis_in, basis_out):
    positions = jnp.arange(LEN, dtype=jnp.int32)[None, :]
    valid_tokens = jnp.logical_and(positions < lengths[:, None], jnp.logical_or(keep_mask == 1, positions == 0)).astype(jnp.float32)
    token_total = jnp.sum(valid_tokens)
    rotated_in = jnp.dot(saved_inputs.reshape(SEQS * LEN, D_IN), basis_in, preferred_element_type=jnp.float32).astype(jnp.bfloat16).reshape(SEQS, LEN, KA)
    grad_sums = jnp.dot(output_grads.reshape(SEQS * LEN, D_OUT), basis_out, preferred_element_type=jnp.float32).reshape(SEQS, LEN, KG)
    rotated_out = (grad_sums * valid_tokens[:, :, None]).astype(jnp.bfloat16)
    squares_sum = jnp.zeros((KG, KA), jnp.float32)
    for seq_index in range(SEQS):
        projected = jnp.dot(rotated_out[seq_index].T, rotated_in[seq_index], preferred_element_type=jnp.float32)
        squares_sum = squares_sum + projected * projected
    return squares_sum / token_total
```

```python
import functools

import jax
import jax.numpy as jnp
from jax import lax
from jax.experimental import pallas as pl
from jax.experimental.pallas import tpu as pltpu
from jax.sharding import PartitionSpec as P

MESH = pl.DeviceIdType.MESH
F32 = jnp.float32
BF16 = jnp.bfloat16
WIDTH = 256
DEPTH = 3
LAG = 2


def rotate_kernel(n, x_ref, g_ref, valid_ref, win_ref, wout_ref, rin_ref, rout_ref,
                  xall, gall, part, from_left, from_right, to_right, to_left, wbuf, wout,
                  pout, csend, crecv, chip, xsend, xrecv, fown, frecv,
                  local_sem, w_sem, xs_sem, xr_sem, gs_sem, gr_sem, hs_sem, hr_sem,
                  rs_sem, rr_sem, ls_sem, lr_sem, os_sem, or_sem):
    num_seqs, slots = x_ref.shape[0], x_ref.shape[1]
    half_cols = chip.shape[1]
    pieces = part.shape[0]
    per_half = pieces // 2
    last = n - 1
    i = lax.axis_index("inp")
    k = lax.axis_index("out")
    xi, ci = lax.div(i, 2), lax.rem(i, 2)
    core = {"inp": xi * 2 + (1 - ci)}
    across = {"inp": (1 - xi) * 2 + ci}
    right = {"out": lax.rem(k + 1, n)}
    left = {"out": lax.rem(k + last, n)}

    def remote(src, dst, send, recv, to):
        return pltpu.make_async_remote_copy(src_ref=src, dst_ref=dst, send_sem=send, recv_sem=recv,
                                            device_id=to, device_id_type=MESH)

    def fetch(t):
        j = lax.rem(t, per_half)
        cols = pl.ds(pl.multiple_of(j * WIDTH, WIDTH), WIDTH)
        slot = lax.rem(t, DEPTH)
        return pltpu.make_async_copy(win_ref.at[:, cols], wbuf.at[slot], w_sem.at[slot])

    own_x = pltpu.make_async_copy(x_ref, xall.at[0, :, 0], local_sem.at[0])
    own_g = pltpu.make_async_copy(g_ref, gall.at[k], local_sem.at[1])
    own_w = pltpu.make_async_copy(wout_ref, wout, local_sem.at[2])
    own_x.start()
    own_g.start()
    own_w.start()
    for t in range(DEPTH - 1):
        fetch(jnp.int32(t)).start()

    barrier = pltpu.get_barrier_semaphore()
    pl.semaphore_signal(barrier, inc=1, device_id=core, device_id_type=MESH)
    pl.semaphore_signal(barrier, inc=1, device_id=across, device_id_type=MESH)

    @pl.when(k > 0)
    def _():
        pl.semaphore_signal(barrier, inc=1, device_id=left, device_id_type=MESH)

    @pl.when(k < last)
    def _():
        pl.semaphore_signal(barrier, inc=1, device_id=right, device_id_type=MESH)

    pl.semaphore_wait(barrier, 4 - jnp.where(k == 0, 1, 0) - jnp.where(k == last, 1, 0))

    x_across = remote(x_ref, xall.at[1, :, 0], xs_sem.at[0], xr_sem.at[0], across)
    x_core = remote(x_ref, xall.at[0, :, 1], xs_sem.at[1], xr_sem.at[1], core)
    x_hand = remote(xall.at[1, :, 0], xall.at[1, :, 1], xs_sem.at[2], xr_sem.at[2], core)
    x_across.start()
    x_core.start()

    def g_right(b):
        return remote(gall.at[b], gall.at[b], gs_sem.at[b], gr_sem.at[b], right)

    def g_left(b):
        return remote(gall.at[b], gall.at[b], hs_sem.at[b], hr_sem.at[b], left)

    own_g.wait()
    for h in range(n):
        lower, upper = k - h, k + h

        @pl.when(lower >= 0)
        def _():
            if h > 0:
                g_right(lower).wait_recv()

            @pl.when(k < last)
            def _():
                g_right(lower).start()

        @pl.when(upper <= last)
        def _():
            if h > 0:
                g_left(upper).wait_recv()

            @pl.when(k > 0)
            def _():
                g_left(upper).start()

    own_w.wait()
    rows = gall.shape[0] * gall.shape[1]
    grads = gall[...].reshape(rows, gall.shape[2])
    for h in range(2):
        pout[h] = jnp.dot(grads, wout[:, h * half_cols:(h + 1) * half_cols], preferred_element_type=F32)
    csend[...] = pout[1 - ci].astype(BF16)
    o_core = remote(csend, crecv, os_sem.at[0], or_sem.at[0], core)
    o_across = remote(xsend, xrecv, os_sem.at[1], or_sem.at[1], across)
    o_final = remote(fown, frecv, os_sem.at[2], or_sem.at[2], core)
    o_core.start()
    own_x.wait()
    x_core.wait_recv()

    def send_right(c):
        return remote(to_right.at[c], from_left.at[c], rs_sem.at[c], rr_sem.at[c], right)

    def send_left(c):
        return remote(to_left.at[c], from_right.at[c], ls_sem.at[c], lr_sem.at[c], left)

    far = jnp.maximum(k, last - k)

    def tick(t, carry):
        @pl.when(t == 2)
        def _():
            o_core.wait_recv()
            chip[...] = pout[ci] + crecv[...].astype(F32)
            xsend[...] = chip[...].astype(BF16)
            o_across.start()

        @pl.when(t == per_half - 4)
        def _():
            x_across.wait_recv()
            x_hand.start()

        @pl.when(t == per_half)
        def _():
            x_hand.wait_recv()

        @pl.when(t == per_half + 4)
        def _():
            o_across.wait_recv()
            fown[...] = ((chip[...] + xrecv[...].astype(F32)) * valid_ref[...]).astype(BF16)
            o_final.start()

        @pl.when(t < pieces)
        def _():
            fetch(t).wait()

            @pl.when(t + DEPTH - 1 < pieces)
            def _():
                fetch(t + DEPTH - 1).start()

            block = xall[lax.div(t, per_half)].reshape(num_seqs * 2 * slots, x_ref.shape[2])
            part[t] = jnp.dot(block, wbuf[lax.rem(t, DEPTH)], preferred_element_type=F32)

        c = t - LAG * k

        @pl.when((c >= 0) & (c < pieces))
        def _():
            @pl.when(k == 0)
            def _():
                to_right[c] = part[c].astype(BF16)

            @pl.when(k > 0)
            def _():
                send_right(c).wait_recv()

                @pl.when(k < last)
                def _():
                    to_right[c] = (part[c] + from_left[c].astype(F32)).astype(BF16)

            @pl.when(k < last)
            def _():
                send_right(c).start()

        d = t - LAG * (last - k)

        @pl.when((d >= 0) & (d < pieces))
        def _():
            @pl.when(k == last)
            def _():
                to_left[d] = part[d].astype(BF16)

            @pl.when(k < last)
            def _():
                send_left(d).wait_recv()

                @pl.when(k > 0)
                def _():
                    to_left[d] = (part[d] + from_right[d].astype(F32)).astype(BF16)

            @pl.when(k > 0)
            def _():
                send_left(d).start()

        e = t - LAG * far

        @pl.when((e >= 0) & (e < pieces))
        def _():
            h, j = lax.div(e, per_half), lax.rem(e, per_half)

            def put(total):
                total = total.astype(BF16)
                for s in range(num_seqs):
                    rin_ref[j, s, h] = total[s * 2 * slots:(s + 1) * 2 * slots]

            @pl.when(k == 0)
            def _():
                put(part[e] + from_right[e].astype(F32))

            @pl.when(k == last)
            def _():
                put(part[e] + from_left[e].astype(F32))

            @pl.when((k > 0) & (k < last))
            def _():
                put(part[e] + from_left[e].astype(F32) + from_right[e].astype(F32))

        return carry

    lax.fori_loop(0, pieces + LAG * last, tick, 0)

    def place(half, ref):
        for b in range(4):
            r = lax.rem(b // 2 + xi, 2) * 2 + lax.rem(b % 2 + ci, 2)
            for s in range(num_seqs):
                first = (b * num_seqs + s) * slots
                rout_ref[half, s, r] = ref[first:first + slots]

    place(ci, fown)
    o_final.wait_recv()
    place(1 - ci, frecv)

    for copy in (x_across, x_core, x_hand, o_core, o_across, o_final):
        copy.wait_send()
    for h in range(n):
        @pl.when((k - h >= 0) & (k < last))
        def _():
            g_right(k - h).wait_send()

        @pl.when((k + h <= last) & (k > 0))
        def _():
            g_left(k + h).wait_send()

    def drain(c, carry):
        @pl.when(k < last)
        def _():
            send_right(c).wait_send()

        @pl.when(k > 0)
        def _():
            send_left(c).wait_send()

        return carry

    lax.fori_loop(0, pieces, drain, 0)


def square_kernel(total_ref, rin_ref, rout_ref, out_ref, turned):
    num_seqs = turned.shape[0]
    rows, half_cols = rout_ref.shape[2] * rout_ref.shape[3], rout_ref.shape[4]

    @pl.when(pl.program_id(0) == 0)
    def _():
        for s in range(num_seqs):
            for h in range(2):
                block = rout_ref[h, s].reshape(rows, half_cols).astype(F32)
                turned[s, h * half_cols:(h + 1) * half_cols] = block.T.astype(BF16)

    total = total_ref[0, 0]
    step = half_cols // 2
    for m in range(turned.shape[1] // step):
        acc = None
        for s in range(num_seqs):
            proj = jnp.dot(turned[s, m * step:(m + 1) * step], rin_ref[0, s], preferred_element_type=F32)
            acc = proj * proj if acc is None else acc + proj * proj
        out_ref[m * step:(m + 1) * step] = acc / total


def token_mask(lengths, keep_mask):
    positions = jnp.arange(keep_mask.shape[1], dtype=jnp.int32)[None, :]
    return jnp.logical_and(
        positions < lengths[:, None], jnp.logical_or(keep_mask == 1, positions == 0)
    ).astype(F32)


def fused_shards(n, saved_inputs, output_grads, lengths, keep_mask, basis_in, basis_out):
    num_seqs, slots, feat = saved_inputs.shape
    gfeat = output_grads.shape[2]
    kin, kout = basis_in.shape[1], basis_out.shape[1]
    rows = num_seqs * slots * 4
    per_half = kin // WIDTH
    pieces = 2 * per_half
    half = rows // 2
    hc = kout // 2
    valid = token_mask(lengths, keep_mask)
    total = jnp.sum(valid).reshape(1, 1)
    column = valid.reshape(num_seqs, 4, slots).transpose(1, 0, 2).reshape(rows, 1)
    dma = pltpu.SemaphoreType.DMA
    anywhere = pl.BlockSpec(memory_space=pl.ANY)
    vmem = pl.BlockSpec(memory_space=pltpu.VMEM)
    rin, rout = pl.pallas_call(
        functools.partial(rotate_kernel, n),
        out_shape=(
            jax.ShapeDtypeStruct((per_half, num_seqs, 2, 2 * slots, WIDTH), BF16),
            jax.ShapeDtypeStruct((2, num_seqs, 4, slots, hc), BF16),
        ),
        in_specs=[anywhere, anywhere, vmem, anywhere, anywhere],
        out_specs=(vmem, vmem),
        scratch_shapes=[
            pltpu.VMEM((2, num_seqs, 2, slots, feat), BF16),
            pltpu.VMEM((n, num_seqs * slots, gfeat), BF16),
            pltpu.VMEM((pieces, half, WIDTH), F32),
            pltpu.VMEM((pieces, half, WIDTH), BF16),
            pltpu.VMEM((pieces, half, WIDTH), BF16),
            pltpu.VMEM((pieces, half, WIDTH), BF16),
            pltpu.VMEM((pieces, half, WIDTH), BF16),
            pltpu.VMEM((DEPTH, feat, WIDTH), BF16),
            pltpu.VMEM((gfeat, kout), BF16),
            pltpu.VMEM((2, rows, hc), F32),
            pltpu.VMEM((rows, hc), BF16),
            pltpu.VMEM((rows, hc), BF16),
            pltpu.VMEM((rows, hc), F32),
            pltpu.VMEM((rows, hc), BF16),
            pltpu.VMEM((rows, hc), BF16),
            pltpu.VMEM((rows, hc), BF16),
            pltpu.VMEM((rows, hc), BF16),
            dma((3,)), dma((DEPTH,)), dma((3,)), dma((3,)),
            dma((n,)), dma((n,)), dma((n,)), dma((n,)),
            dma((pieces,)), dma((pieces,)), dma((pieces,)), dma((pieces,)),
            dma((3,)), dma((3,)),
        ],
        compiler_params=pltpu.CompilerParams(
            collective_id=0, has_side_effects=True, vmem_limit_bytes=60 * 1024 * 1024
        ),
        cost_estimate=pl.CostEstimate(
            flops=2 * rows * (feat * kin + gfeat * kout), bytes_accessed=4 * feat * kin, transcendentals=0
        ),
        name="rotate",
    )(saved_inputs, output_grads.reshape(num_seqs * slots, gfeat), column, basis_in, basis_out)
    rin = rin.reshape(per_half, num_seqs, 4 * slots, WIDTH)
    return pl.pallas_call(
        square_kernel,
        grid=(per_half,),
        out_shape=jax.ShapeDtypeStruct((kout, kin), F32),
        in_specs=[
            pl.BlockSpec(memory_space=pltpu.SMEM),
            pl.BlockSpec((1, num_seqs, 4 * slots, WIDTH), lambda j: (j, 0, 0, 0)),
            pl.BlockSpec((2, num_seqs, 4, slots, hc), lambda j: (0, 0, 0, 0, 0)),
        ],
        out_specs=pl.BlockSpec((kout, WIDTH), lambda j: (0, j)),
        scratch_shapes=[pltpu.VMEM((num_seqs, kout, 4 * slots), BF16)],
        compiler_params=pltpu.CompilerParams(vmem_limit_bytes=32 * 1024 * 1024),
        cost_estimate=pl.CostEstimate(
            flops=2 * rows * kin * kout, bytes_accessed=4 * kin * kout, transcendentals=0
        ),
        name="square",
    )(total, rin, rout)


def plain_shards(saved_inputs, output_grads, lengths, keep_mask, basis_in, basis_out):
    num_seqs = saved_inputs.shape[0]
    seq_slots = keep_mask.shape[1]
    rows_all = num_seqs * seq_slots
    valid_tokens = token_mask(lengths, keep_mask)
    token_total = jnp.sum(valid_tokens)
    gathered_inputs = lax.all_gather(saved_inputs, "inp", axis=1, tiled=True)
    flat_inputs = gathered_inputs.reshape(rows_all, gathered_inputs.shape[2])
    partial_in = jnp.dot(flat_inputs, basis_in, preferred_element_type=F32)
    rotated_in = lax.psum(partial_in, "out").astype(BF16)
    rotated_in = rotated_in.reshape(num_seqs, seq_slots, basis_in.shape[1])
    gathered_grads = lax.all_gather(output_grads, "out", axis=1, tiled=True)
    flat_grads = gathered_grads.reshape(rows_all, gathered_grads.shape[2])
    partial_out = jnp.dot(flat_grads, basis_out, preferred_element_type=F32)
    grad_sums = lax.psum(partial_out, "inp")
    grad_sums = grad_sums.reshape(num_seqs, seq_slots, basis_out.shape[1])
    rotated_out = (grad_sums * valid_tokens[:, :, None]).astype(BF16)
    projected = jnp.einsum("stg,sta->sga", rotated_out, rotated_in, preferred_element_type=F32)
    return jnp.sum(projected * projected, axis=0) / token_total


def solution(mesh):
    in_specs = (
        P("grp", "inp", "out"),
        P("grp", "out", "inp"),
        P("grp"),
        P("grp", None),
        P("out", "inp"),
        P("inp", "out"),
    )
    out_specs = P(("grp", "out"), "inp")
    if mesh.shape["inp"] == 4 and mesh.shape["out"] == 4:
        body = functools.partial(fused_shards, mesh.shape["out"])
    else:
        body = plain_shards
    return jax.shard_map(body, mesh=mesh, in_specs=in_specs, out_specs=out_specs, check_vma=False)
```

```python
import functools

import jax
import jax.numpy as jnp
from jax import lax
from jax.experimental import pallas as pl
from jax.experimental.pallas import tpu as pltpu
from jax.sharding import PartitionSpec as P

MESH = pl.DeviceIdType.MESH
F32 = jnp.float32
BF16 = jnp.bfloat16
WIDTH = 256
HOP = 2
DEPTH = 3
LAG = 2


def rotate_kernel(n, x_ref, g_ref, win_ref, wout_ref, rin_ref, rout_ref,
                  xall, gall, part, from_left, from_right, to_right, to_left, wbuf, wout,
                  pout, crecv, chip, xrecv, fown, frecv,
                  local_sem, w_sem, xs_sem, xr_sem, gs_sem, gr_sem, hs_sem, hr_sem,
                  rs_sem, rr_sem, ls_sem, lr_sem, os_sem, or_sem):
    num_seqs, slots = x_ref.shape[0], x_ref.shape[1]
    half_cols = chip.shape[1]
    pieces = part.shape[0]
    per_half = pieces // 2
    last = n - 1
    i = lax.axis_index("inp")
    k = lax.axis_index("out")
    xi, ci = lax.div(i, 2), lax.rem(i, 2)
    core = {"inp": xi * 2 + (1 - ci)}
    across = {"inp": (1 - xi) * 2 + ci}
    right = {"out": lax.rem(k + 1, n)}
    left = {"out": lax.rem(k + last, n)}

    def remote(src, dst, send, recv, to):
        return pltpu.make_async_remote_copy(src_ref=src, dst_ref=dst, send_sem=send, recv_sem=recv,
                                            device_id=to, device_id_type=MESH)

    def fetch(t):
        j = lax.rem(t, per_half)
        cols = pl.ds(pl.multiple_of(j * WIDTH, WIDTH), WIDTH)
        slot = lax.rem(t, DEPTH)
        return pltpu.make_async_copy(win_ref.at[:, cols], wbuf.at[slot], w_sem.at[slot])

    own_x = pltpu.make_async_copy(x_ref, xall.at[0, :, ci], local_sem.at[0])
    own_g = pltpu.make_async_copy(g_ref, gall.at[k], local_sem.at[1])
    own_w = pltpu.make_async_copy(wout_ref, wout, local_sem.at[2])
    own_x.start()
    own_g.start()
    own_w.start()
    for t in range(DEPTH - 1):
        fetch(jnp.int32(t)).start()

    barrier = pltpu.get_barrier_semaphore()
    pl.semaphore_signal(barrier, inc=1, device_id=core, device_id_type=MESH)
    pl.semaphore_signal(barrier, inc=1, device_id=across, device_id_type=MESH)

    @pl.when(k > 0)
    def _():
        pl.semaphore_signal(barrier, inc=1, device_id=left, device_id_type=MESH)

    @pl.when(k < last)
    def _():
        pl.semaphore_signal(barrier, inc=1, device_id=right, device_id_type=MESH)

    pl.semaphore_wait(barrier, 4 - jnp.where(k == 0, 1, 0) - jnp.where(k == last, 1, 0))

    x_across = remote(x_ref, xall.at[1, :, ci], xs_sem.at[0], xr_sem.at[0], across)
    x_core = remote(x_ref, xall.at[0, :, ci], xs_sem.at[1], xr_sem.at[1], core)
    x_hand = remote(xall.at[1, :, ci], xall.at[1, :, ci], xs_sem.at[2], xr_sem.at[2], core)
    def g_right(b):
        return remote(gall.at[b], gall.at[b], gs_sem.at[b], gr_sem.at[b], right)

    def g_left(b):
        return remote(gall.at[b], gall.at[b], hs_sem.at[b], hr_sem.at[b], left)

    def pass_grads(h):
        lower, upper = k - h, k + h

        @pl.when(lower >= 0)
        def _():
            if h > 0:
                g_right(lower).wait_recv()

            @pl.when(k < last)
            def _():
                g_right(lower).start()

        @pl.when(upper <= last)
        def _():
            if h > 0:
                g_left(upper).wait_recv()

            @pl.when(k > 0)
            def _():
                g_left(upper).start()

    own_g.wait()
    pass_grads(0)
    x_core.start()
    x_across.start()

    o_core = remote(pout.at[1 - ci], crecv, os_sem.at[0], or_sem.at[0], core)
    o_across = remote(chip, xrecv, os_sem.at[1], or_sem.at[1], across)
    o_final = remote(fown, frecv, os_sem.at[2], or_sem.at[2], core)
    own_x.wait()
    x_core.wait_recv()

    def send_right(c):
        return remote(to_right.at[c], from_left.at[c], rs_sem.at[c], rr_sem.at[c], right)

    def send_left(c):
        return remote(to_left.at[c], from_right.at[c], ls_sem.at[c], lr_sem.at[c], left)

    far = jnp.maximum(k, last - k)

    def tick(t, carry):
        for h in range(1, n):
            @pl.when(t == HOP * h)
            def _():
                pass_grads(h)

        @pl.when(t == HOP * n)
        def _():
            own_w.wait()
            grads = gall[...].reshape(gall.shape[0] * gall.shape[1], gall.shape[2])
            for h in range(2):
                pout[h] = jnp.dot(grads, wout[:, h * half_cols:(h + 1) * half_cols], preferred_element_type=F32)
            o_core.start()

        @pl.when(t == HOP * n + 1)
        def _():
            o_core.wait_recv()
            chip[...] = pout[ci] + crecv[...]
            o_across.start()

        @pl.when(t == per_half - 3)
        def _():
            x_across.wait_recv()
            x_hand.start()

        @pl.when(t == per_half)
        def _():
            x_hand.wait_recv()

        @pl.when(t == pieces - 1)
        def _():
            o_across.wait_recv()
            fown[...] = (chip[...] + xrecv[...]).astype(BF16)
            o_final.start()

        @pl.when(t < pieces)
        def _():
            fetch(t).wait()

            @pl.when(t + DEPTH - 1 < pieces)
            def _():
                fetch(t + DEPTH - 1).start()

            block = xall[lax.div(t, per_half)].reshape(num_seqs * 2 * slots, x_ref.shape[2])
            part[t] = jnp.dot(block, wbuf[lax.rem(t, DEPTH)], preferred_element_type=F32)

        c = t - LAG * k

        @pl.when((c >= 0) & (c < pieces))
        def _():
            @pl.when(k == 0)
            def _():
                to_right[c] = part[c].astype(BF16)

            @pl.when(k > 0)
            def _():
                send_right(c).wait_recv()

                @pl.when(k < last)
                def _():
                    to_right[c] = (part[c] + from_left[c].astype(F32)).astype(BF16)

            @pl.when(k < last)
            def _():
                send_right(c).start()

        d = t - LAG * (last - k)

        @pl.when((d >= 0) & (d < pieces))
        def _():
            @pl.when(k == last)
            def _():
                to_left[d] = part[d].astype(BF16)

            @pl.when(k < last)
            def _():
                send_left(d).wait_recv()

                @pl.when(k > 0)
                def _():
                    to_left[d] = (part[d] + from_right[d].astype(F32)).astype(BF16)

            @pl.when(k > 0)
            def _():
                send_left(d).start()

        e = t - LAG * far

        @pl.when((e >= 0) & (e < pieces))
        def _():
            h, j = lax.div(e, per_half), lax.rem(e, per_half)

            def put(total):
                total = total.astype(BF16)
                for s in range(num_seqs):
                    rin_ref[j, s, lax.rem(xi + h, 2)] = total[s * 2 * slots:(s + 1) * 2 * slots]

            @pl.when(k == 0)
            def _():
                put(part[e] + from_right[e].astype(F32))

            @pl.when(k == last)
            def _():
                put(part[e] + from_left[e].astype(F32))

            @pl.when((k > 0) & (k < last))
            def _():
                put(part[e] + from_left[e].astype(F32) + from_right[e].astype(F32))

        return carry

    lax.fori_loop(0, pieces + LAG * last, tick, 0)

    rout_ref[ci] = fown[...]
    o_final.wait_recv()
    rout_ref[1 - ci] = frecv[...]

    for copy in (x_across, x_core, x_hand, o_core, o_across, o_final):
        copy.wait_send()
    for h in range(n):
        @pl.when((k - h >= 0) & (k < last))
        def _():
            g_right(k - h).wait_send()

        @pl.when((k + h <= last) & (k > 0))
        def _():
            g_left(k + h).wait_send()

    def drain(c, carry):
        @pl.when(k < last)
        def _():
            send_right(c).wait_send()

        @pl.when(k > 0)
        def _():
            send_left(c).wait_send()

        return carry

    lax.fori_loop(0, pieces, drain, 0)


def square_kernel(lengths_ref, keep_ref, rin_ref, rout_ref, out_ref, turned, scale):
    num_seqs, _, seq_slots = turned.shape
    half_cols = rout_ref.shape[4]

    @pl.when(pl.program_id(0) == 0)
    def _():
        slot = lax.broadcasted_iota(jnp.int32, (1, seq_slots), 1)
        total = jnp.float32(0)
        for s in range(num_seqs):
            kept = (keep_ref[s:s + 1] == 1) | (slot == 0)
            valid = jnp.where((slot < lengths_ref[s]) & kept, 1.0, 0.0).astype(F32)
            total += jnp.sum(valid)
            for h in range(2):
                block = rout_ref[h, :, s].reshape(seq_slots, half_cols).astype(F32)
                turned[s, h * half_cols:(h + 1) * half_cols] = (block.T * valid).astype(BF16)
        scale[0] = total

    share = 1.0 / jnp.full((1, out_ref.shape[1]), scale[0], F32)
    step = half_cols // 2
    for m in range(turned.shape[1] // step):
        acc = None
        for s in range(num_seqs):
            proj = jnp.dot(turned[s, m * step:(m + 1) * step], rin_ref[0, s], preferred_element_type=F32)
            acc = proj * proj if acc is None else acc + proj * proj
        out_ref[m * step:(m + 1) * step] = acc * share


def token_mask(lengths, keep_mask):
    positions = jnp.arange(keep_mask.shape[1], dtype=jnp.int32)[None, :]
    return jnp.logical_and(
        positions < lengths[:, None], jnp.logical_or(keep_mask == 1, positions == 0)
    ).astype(F32)


def fused_shards(n, saved_inputs, output_grads, lengths, keep_mask, basis_in, basis_out):
    num_seqs, slots, feat = saved_inputs.shape
    gfeat = output_grads.shape[2]
    kin, kout = basis_in.shape[1], basis_out.shape[1]
    rows = num_seqs * slots * 4
    per_half = kin // WIDTH
    pieces = 2 * per_half
    half = rows // 2
    hc = kout // 2
    dma = pltpu.SemaphoreType.DMA
    anywhere = pl.BlockSpec(memory_space=pl.ANY)
    vmem = pl.BlockSpec(memory_space=pltpu.VMEM)
    rin, rout = pl.pallas_call(
        functools.partial(rotate_kernel, n),
        out_shape=(
            jax.ShapeDtypeStruct((per_half, num_seqs, 2, 2 * slots, WIDTH), BF16),
            jax.ShapeDtypeStruct((2, rows, hc), BF16),
        ),
        in_specs=[anywhere] * 4,
        out_specs=(vmem, vmem),
        scratch_shapes=[
            pltpu.VMEM((2, num_seqs, 2, slots, feat), BF16),
            pltpu.VMEM((n, num_seqs * slots, gfeat), BF16),
            pltpu.VMEM((pieces, half, WIDTH), F32),
            pltpu.VMEM((pieces, half, WIDTH), BF16),
            pltpu.VMEM((pieces, half, WIDTH), BF16),
            pltpu.VMEM((pieces, half, WIDTH), BF16),
            pltpu.VMEM((pieces, half, WIDTH), BF16),
            pltpu.VMEM((DEPTH, feat, WIDTH), BF16),
            pltpu.VMEM((gfeat, kout), BF16),
            pltpu.VMEM((2, rows, hc), F32),
            pltpu.VMEM((rows, hc), F32),
            pltpu.VMEM((rows, hc), F32),
            pltpu.VMEM((rows, hc), F32),
            pltpu.VMEM((rows, hc), BF16),
            pltpu.VMEM((rows, hc), BF16),
            dma((3,)), dma((DEPTH,)), dma((3,)), dma((3,)),
            dma((n,)), dma((n,)), dma((n,)), dma((n,)),
            dma((pieces,)), dma((pieces,)), dma((pieces,)), dma((pieces,)),
            dma((3,)), dma((3,)),
        ],
        compiler_params=pltpu.CompilerParams(
            collective_id=0, has_side_effects=True, vmem_limit_bytes=60 * 1024 * 1024
        ),
        cost_estimate=pl.CostEstimate(
            flops=2 * rows * (feat * kin + gfeat * kout), bytes_accessed=4 * feat * kin, transcendentals=0
        ),
        name="rotate",
    )(saved_inputs, output_grads.reshape(num_seqs * slots, gfeat), basis_in, basis_out)
    rin = rin.reshape(per_half, num_seqs, 4 * slots, WIDTH)
    rout = rout.reshape(2, 4, num_seqs, slots, hc)
    return pl.pallas_call(
        square_kernel,
        grid=(per_half,),
        out_shape=jax.ShapeDtypeStruct((kout, kin), F32),
        in_specs=[
            pl.BlockSpec(memory_space=pltpu.SMEM),
            pl.BlockSpec((num_seqs, 4 * slots), lambda j: (0, 0)),
            pl.BlockSpec((1, num_seqs, 4 * slots, WIDTH), lambda j: (j, 0, 0, 0)),
            pl.BlockSpec((2, 4, num_seqs, slots, hc), lambda j: (0, 0, 0, 0, 0)),
        ],
        out_specs=pl.BlockSpec((kout, WIDTH), lambda j: (0, j)),
        scratch_shapes=[pltpu.VMEM((num_seqs, kout, 4 * slots), BF16), pltpu.SMEM((1,), F32)],
        compiler_params=pltpu.CompilerParams(vmem_limit_bytes=60 * 1024 * 1024),
        cost_estimate=pl.CostEstimate(
            flops=2 * rows * kin * kout, bytes_accessed=4 * kin * kout, transcendentals=0
        ),
        name="square",
    )(lengths, keep_mask, rin, rout)


def plain_shards(saved_inputs, output_grads, lengths, keep_mask, basis_in, basis_out):
    num_seqs = saved_inputs.shape[0]
    seq_slots = keep_mask.shape[1]
    rows_all = num_seqs * seq_slots
    valid_tokens = token_mask(lengths, keep_mask)
    token_total = jnp.sum(valid_tokens)
    gathered_inputs = lax.all_gather(saved_inputs, "inp", axis=1, tiled=True)
    flat_inputs = gathered_inputs.reshape(rows_all, gathered_inputs.shape[2])
    partial_in = jnp.dot(flat_inputs, basis_in, preferred_element_type=F32)
    rotated_in = lax.psum(partial_in, "out").astype(BF16)
    rotated_in = rotated_in.reshape(num_seqs, seq_slots, basis_in.shape[1])
    gathered_grads = lax.all_gather(output_grads, "out", axis=1, tiled=True)
    flat_grads = gathered_grads.reshape(rows_all, gathered_grads.shape[2])
    partial_out = jnp.dot(flat_grads, basis_out, preferred_element_type=F32)
    grad_sums = lax.psum(partial_out, "inp")
    grad_sums = grad_sums.reshape(num_seqs, seq_slots, basis_out.shape[1])
    rotated_out = (grad_sums * valid_tokens[:, :, None]).astype(BF16)
    projected = jnp.einsum("stg,sta->sga", rotated_out, rotated_in, preferred_element_type=F32)
    return jnp.sum(projected * projected, axis=0) / token_total


def solution(mesh):
    in_specs = (
        P("grp", "inp", "out"),
        P("grp", "out", "inp"),
        P("grp"),
        P("grp", None),
        P("out", "inp"),
        P("inp", "out"),
    )
    out_specs = P(("grp", "out"), "inp")
    if mesh.shape["inp"] == 4 and mesh.shape["out"] == 4:
        body = functools.partial(fused_shards, mesh.shape["out"])
    else:
        body = plain_shards
    return jax.shard_map(body, mesh=mesh, in_specs=in_specs, out_specs=out_specs, check_vma=False)
```

```python
import functools

import jax
import jax.numpy as jnp
from jax import lax
from jax.experimental import pallas as pl
from jax.experimental.pallas import tpu as pltpu
from jax.sharding import PartitionSpec as P

MESH = pl.DeviceIdType.MESH
F32 = jnp.float32
BF16 = jnp.bfloat16
WIDTH = 256
HOP = 2
DEPTH = 3
LAG = 2


def rotate_kernel(n, x_ref, g_ref, win_ref, wout_ref, rin_ref, rout_ref,
                  xall, gall, part, from_left, from_right, to_right, to_left, wbuf, wout,
                  pout, crecv, chip, xrecv, fown, frecv,
                  local_sem, w_sem, xs_sem, xr_sem, gs_sem, gr_sem, hs_sem, hr_sem,
                  rs_sem, rr_sem, ls_sem, lr_sem, os_sem, or_sem):
    num_seqs, slots = x_ref.shape[0], x_ref.shape[1]
    half_cols = chip.shape[1]
    pieces = part.shape[0]
    per_half = pieces // 2
    last = n - 1
    i = lax.axis_index("inp")
    k = lax.axis_index("out")
    xi, ci = lax.div(i, 2), lax.rem(i, 2)
    core = {"inp": xi * 2 + (1 - ci)}
    across = {"inp": (1 - xi) * 2 + ci}
    right = {"out": lax.rem(k + 1, n)}
    left = {"out": lax.rem(k + last, n)}

    def remote(src, dst, send, recv, to):
        return pltpu.make_async_remote_copy(src_ref=src, dst_ref=dst, send_sem=send, recv_sem=recv,
                                            device_id=to, device_id_type=MESH)

    def fetch(t):
        j = lax.rem(t, per_half)
        cols = pl.ds(pl.multiple_of(j * WIDTH, WIDTH), WIDTH)
        slot = lax.rem(t, DEPTH)
        return pltpu.make_async_copy(win_ref.at[:, cols], wbuf.at[slot], w_sem.at[slot])

    own_x = pltpu.make_async_copy(x_ref, xall.at[0, :, ci], local_sem.at[0])
    own_g = pltpu.make_async_copy(g_ref, gall.at[k], local_sem.at[1])
    own_w = pltpu.make_async_copy(wout_ref, wout, local_sem.at[2])
    own_x.start()
    own_g.start()
    own_w.start()
    for t in range(DEPTH - 1):
        fetch(jnp.int32(t)).start()

    barrier = pltpu.get_barrier_semaphore()
    pl.semaphore_signal(barrier, inc=1, device_id=core, device_id_type=MESH)
    pl.semaphore_signal(barrier, inc=1, device_id=across, device_id_type=MESH)

    @pl.when(k > 0)
    def _():
        pl.semaphore_signal(barrier, inc=1, device_id=left, device_id_type=MESH)

    @pl.when(k < last)
    def _():
        pl.semaphore_signal(barrier, inc=1, device_id=right, device_id_type=MESH)

    pl.semaphore_wait(barrier, 4 - jnp.where(k == 0, 1, 0) - jnp.where(k == last, 1, 0))

    x_across = remote(x_ref, xall.at[1, :, ci], xs_sem.at[0], xr_sem.at[0], across)
    x_core = remote(x_ref, xall.at[0, :, ci], xs_sem.at[1], xr_sem.at[1], core)
    x_hand = remote(xall.at[1, :, ci], xall.at[1, :, ci], xs_sem.at[2], xr_sem.at[2], core)
    def g_right(b):
        return remote(gall.at[b], gall.at[b], gs_sem.at[b], gr_sem.at[b], right)

    def g_left(b):
        return remote(gall.at[b], gall.at[b], hs_sem.at[b], hr_sem.at[b], left)

    def pass_grads(h):
        lower, upper = k - h, k + h

        @pl.when(lower >= 0)
        def _():
            if h > 0:
                g_right(lower).wait_recv()

            @pl.when(k < last)
            def _():
                g_right(lower).start()

        @pl.when(upper <= last)
        def _():
            if h > 0:
                g_left(upper).wait_recv()

            @pl.when(k > 0)
            def _():
                g_left(upper).start()

    x_across.start()
    own_g.wait()
    pass_grads(0)
    x_core.start()

    o_core = remote(pout.at[1 - ci], crecv, os_sem.at[0], or_sem.at[0], core)
    o_across = remote(chip, xrecv, os_sem.at[1], or_sem.at[1], across)
    o_final = remote(fown, frecv, os_sem.at[2], or_sem.at[2], core)
    own_x.wait()
    x_core.wait_recv()

    def send_right(c):
        return remote(to_right.at[c], from_left.at[c], rs_sem.at[c], rr_sem.at[c], right)

    def send_left(c):
        return remote(to_left.at[c], from_right.at[c], ls_sem.at[c], lr_sem.at[c], left)

    far = jnp.maximum(k, last - k)

    def tick(t, carry):
        for h in range(1, n):
            @pl.when(t == HOP * h)
            def _():
                pass_grads(h)

        @pl.when(t == HOP * n)
        def _():
            own_w.wait()
            grads = gall[...].reshape(gall.shape[0] * gall.shape[1], gall.shape[2])
            for h in range(2):
                pout[h] = jnp.dot(grads, wout[:, h * half_cols:(h + 1) * half_cols], preferred_element_type=F32)
            o_core.start()

        @pl.when(t == HOP * n + 1)
        def _():
            o_core.wait_recv()
            chip[...] = pout[ci] + crecv[...]

        @pl.when(t == per_half - 2)
        def _():
            x_across.wait_recv()
            x_hand.start()
            o_across.start()

        @pl.when(t == per_half)
        def _():
            x_hand.wait_recv()

        @pl.when(t == pieces - 1)
        def _():
            o_across.wait_recv()
            fown[...] = (chip[...] + xrecv[...]).astype(BF16)
            o_final.start()

        @pl.when(t < pieces)
        def _():
            fetch(t).wait()

            @pl.when(t + DEPTH - 1 < pieces)
            def _():
                fetch(t + DEPTH - 1).start()

            block = xall[lax.div(t, per_half)].reshape(num_seqs * 2 * slots, x_ref.shape[2])
            part[t] = jnp.dot(block, wbuf[lax.rem(t, DEPTH)], preferred_element_type=F32)

        c = t - LAG * k

        @pl.when((c >= 0) & (c < pieces))
        def _():
            @pl.when(k == 0)
            def _():
                to_right[c] = part[c].astype(BF16)

            @pl.when(k > 0)
            def _():
                send_right(c).wait_recv()

                @pl.when(k < last)
                def _():
                    to_right[c] = (part[c] + from_left[c].astype(F32)).astype(BF16)

            @pl.when(k < last)
            def _():
                send_right(c).start()

        d = t - LAG * (last - k)

        @pl.when((d >= 0) & (d < pieces))
        def _():
            @pl.when(k == last)
            def _():
                to_left[d] = part[d].astype(BF16)

            @pl.when(k < last)
            def _():
                send_left(d).wait_recv()

                @pl.when(k > 0)
                def _():
                    to_left[d] = (part[d] + from_right[d].astype(F32)).astype(BF16)

            @pl.when(k > 0)
            def _():
                send_left(d).start()

        e = t - LAG * far

        @pl.when((e >= 0) & (e < pieces))
        def _():
            h, j = lax.div(e, per_half), lax.rem(e, per_half)

            def put(total):
                total = total.astype(BF16)
                for s in range(num_seqs):
                    rin_ref[j, s, lax.rem(xi + h, 2)] = total[s * 2 * slots:(s + 1) * 2 * slots]

            @pl.when(k == 0)
            def _():
                put(part[e] + from_right[e].astype(F32))

            @pl.when(k == last)
            def _():
                put(part[e] + from_left[e].astype(F32))

            @pl.when((k > 0) & (k < last))
            def _():
                put(part[e] + from_left[e].astype(F32) + from_right[e].astype(F32))

        return carry

    lax.fori_loop(0, pieces + LAG * last, tick, 0)

    rout_ref[ci] = fown[...]
    o_final.wait_recv()
    rout_ref[1 - ci] = frecv[...]

    for copy in (x_across, x_core, x_hand, o_core, o_across, o_final):
        copy.wait_send()
    for h in range(n):
        @pl.when((k - h >= 0) & (k < last))
        def _():
            g_right(k - h).wait_send()

        @pl.when((k + h <= last) & (k > 0))
        def _():
            g_left(k + h).wait_send()

    def drain(c, carry):
        @pl.when(k < last)
        def _():
            send_right(c).wait_send()

        @pl.when(k > 0)
        def _():
            send_left(c).wait_send()

        return carry

    lax.fori_loop(0, pieces, drain, 0)


def square_kernel(lengths_ref, keep_ref, rin_ref, rout_ref, out_ref, turned, scale):
    num_seqs, _, seq_slots = turned.shape
    half_cols = rout_ref.shape[4]

    @pl.when(pl.program_id(0) == 0)
    def _():
        slot = lax.broadcasted_iota(jnp.int32, (1, seq_slots), 1)
        total = jnp.float32(0)
        for s in range(num_seqs):
            kept = (keep_ref[s:s + 1] == 1) | (slot == 0)
            valid = jnp.where((slot < lengths_ref[s]) & kept, 1.0, 0.0).astype(F32)
            total += jnp.sum(valid)
            for h in range(2):
                block = rout_ref[h, :, s].reshape(seq_slots, half_cols).astype(F32)
                turned[s, h * half_cols:(h + 1) * half_cols] = (block.T * valid).astype(BF16)
        scale[0] = total

    share = 1.0 / jnp.full((1, rin_ref.shape[3]), scale[0], F32)
    step = half_cols // 2
    for q in range(rin_ref.shape[0]):
        wide = rin_ref.shape[3]
        for m in range(turned.shape[1] // step):
            acc = None
            for s in range(num_seqs):
                proj = jnp.dot(turned[s, m * step:(m + 1) * step], rin_ref[q, s], preferred_element_type=F32)
                acc = proj * proj if acc is None else acc + proj * proj
            out_ref[m * step:(m + 1) * step, q * wide:(q + 1) * wide] = acc * share


def token_mask(lengths, keep_mask):
    positions = jnp.arange(keep_mask.shape[1], dtype=jnp.int32)[None, :]
    return jnp.logical_and(
        positions < lengths[:, None], jnp.logical_or(keep_mask == 1, positions == 0)
    ).astype(F32)


def fused_shards(n, saved_inputs, output_grads, lengths, keep_mask, basis_in, basis_out):
    num_seqs, slots, feat = saved_inputs.shape
    gfeat = output_grads.shape[2]
    kin, kout = basis_in.shape[1], basis_out.shape[1]
    rows = num_seqs * slots * 4
    per_half = kin // WIDTH
    pieces = 2 * per_half
    half = rows // 2
    hc = kout // 2
    dma = pltpu.SemaphoreType.DMA
    anywhere = pl.BlockSpec(memory_space=pl.ANY)
    vmem = pl.BlockSpec(memory_space=pltpu.VMEM)
    rin, rout = pl.pallas_call(
        functools.partial(rotate_kernel, n),
        out_shape=(
            jax.ShapeDtypeStruct((per_half, num_seqs, 2, 2 * slots, WIDTH), BF16),
            jax.ShapeDtypeStruct((2, rows, hc), BF16),
        ),
        in_specs=[anywhere] * 4,
        out_specs=(vmem, vmem),
        scratch_shapes=[
            pltpu.VMEM((2, num_seqs, 2, slots, feat), BF16),
            pltpu.VMEM((n, num_seqs * slots, gfeat), BF16),
            pltpu.VMEM((pieces, half, WIDTH), F32),
            pltpu.VMEM((pieces, half, WIDTH), BF16),
            pltpu.VMEM((pieces, half, WIDTH), BF16),
            pltpu.VMEM((pieces, half, WIDTH), BF16),
            pltpu.VMEM((pieces, half, WIDTH), BF16),
            pltpu.VMEM((DEPTH, feat, WIDTH), BF16),
            pltpu.VMEM((gfeat, kout), BF16),
            pltpu.VMEM((2, rows, hc), F32),
            pltpu.VMEM((rows, hc), F32),
            pltpu.VMEM((rows, hc), F32),
            pltpu.VMEM((rows, hc), F32),
            pltpu.VMEM((rows, hc), BF16),
            pltpu.VMEM((rows, hc), BF16),
            dma((3,)), dma((DEPTH,)), dma((3,)), dma((3,)),
            dma((n,)), dma((n,)), dma((n,)), dma((n,)),
            dma((pieces,)), dma((pieces,)), dma((pieces,)), dma((pieces,)),
            dma((3,)), dma((3,)),
        ],
        compiler_params=pltpu.CompilerParams(
            collective_id=0, has_side_effects=True, vmem_limit_bytes=60 * 1024 * 1024
        ),
        cost_estimate=pl.CostEstimate(
            flops=2 * rows * (feat * kin + gfeat * kout), bytes_accessed=4 * feat * kin, transcendentals=0
        ),
        name="rotate",
    )(saved_inputs, output_grads.reshape(num_seqs * slots, gfeat), basis_in, basis_out)
    rin = rin.reshape(per_half, num_seqs, 4 * slots, WIDTH)
    rout = rout.reshape(2, 4, num_seqs, slots, hc)
    return pl.pallas_call(
        square_kernel,
        grid=(per_half // 2,),
        out_shape=jax.ShapeDtypeStruct((kout, kin), F32),
        in_specs=[
            pl.BlockSpec(memory_space=pltpu.SMEM),
            pl.BlockSpec((num_seqs, 4 * slots), lambda j: (0, 0)),
            pl.BlockSpec((2, num_seqs, 4 * slots, WIDTH), lambda j: (j, 0, 0, 0)),
            pl.BlockSpec((2, 4, num_seqs, slots, hc), lambda j: (0, 0, 0, 0, 0)),
        ],
        out_specs=pl.BlockSpec((kout, 2 * WIDTH), lambda j: (0, j)),
        scratch_shapes=[pltpu.VMEM((num_seqs, kout, 4 * slots), BF16), pltpu.SMEM((1,), F32)],
        compiler_params=pltpu.CompilerParams(vmem_limit_bytes=60 * 1024 * 1024),
        cost_estimate=pl.CostEstimate(
            flops=2 * rows * kin * kout, bytes_accessed=4 * kin * kout, transcendentals=0
        ),
        name="square",
    )(lengths, keep_mask, rin, rout)


def plain_shards(saved_inputs, output_grads, lengths, keep_mask, basis_in, basis_out):
    num_seqs = saved_inputs.shape[0]
    seq_slots = keep_mask.shape[1]
    rows_all = num_seqs * seq_slots
    valid_tokens = token_mask(lengths, keep_mask)
    token_total = jnp.sum(valid_tokens)
    gathered_inputs = lax.all_gather(saved_inputs, "inp", axis=1, tiled=True)
    flat_inputs = gathered_inputs.reshape(rows_all, gathered_inputs.shape[2])
    partial_in = jnp.dot(flat_inputs, basis_in, preferred_element_type=F32)
    rotated_in = lax.psum(partial_in, "out").astype(BF16)
    rotated_in = rotated_in.reshape(num_seqs, seq_slots, basis_in.shape[1])
    gathered_grads = lax.all_gather(output_grads, "out", axis=1, tiled=True)
    flat_grads = gathered_grads.reshape(rows_all, gathered_grads.shape[2])
    partial_out = jnp.dot(flat_grads, basis_out, preferred_element_type=F32)
    grad_sums = lax.psum(partial_out, "inp")
    grad_sums = grad_sums.reshape(num_seqs, seq_slots, basis_out.shape[1])
    rotated_out = (grad_sums * valid_tokens[:, :, None]).astype(BF16)
    projected = jnp.einsum("stg,sta->sga", rotated_out, rotated_in, preferred_element_type=F32)
    return jnp.sum(projected * projected, axis=0) / token_total


def solution(mesh):
    in_specs = (
        P("grp", "inp", "out"),
        P("grp", "out", "inp"),
        P("grp"),
        P("grp", None),
        P("out", "inp"),
        P("inp", "out"),
    )
    out_specs = P(("grp", "out"), "inp")
    if mesh.shape["inp"] == 4 and mesh.shape["out"] == 4:
        body = functools.partial(fused_shards, mesh.shape["out"])
    else:
        body = plain_shards
    return jax.shard_map(body, mesh=mesh, in_specs=in_specs, out_specs=out_specs, check_vma=False)
```
